512 devices in a mesh: dp: 8 (over y, core), seq: 16 (over x, z_lo), mp: 4 (over z_hi).
Axes of the slice: x: 4, y: 4, z: 16 (z_hi: 4, z_lo: 4; z = z_hi * 4 + z_lo), core: 2. Of those that a mesh axis runs over, the one named last changes fastest.
Arguments:
- query: bfloat16 [8, 2560, 1536], P('dp', 'seq'), may hold values from -8 to 8
- key: bfloat16 [8, 2560, 1536], P('dp', 'seq'), may hold values from -8 to 8
- value: bfloat16 [8, 2560, 1536], P('dp', 'seq'), may hold values from -6 to 6
- proj_weight: bfloat16 [1536, 1536], P(None, 'mp'), may hold values from -0.15625 to 0.15625
- grad_out: bfloat16 [8, 2560, 1536], P('dp', 'seq', 'mp'), may hold values from -6 to 6
Outputs:
- attended: bfloat16 [8, 2560, 1536], P('dp', 'seq', 'mp')
- grad_query: bfloat16 [8, 2560, 1536], P('dp', ('seq', 'mp'))
- grad_key: bfloat16 [8, 2560, 1536], P('dp', ('seq', 'mp'))
- grad_value: bfloat16 [8, 2560, 1536], P('dp', ('seq', 'mp'))
- grad_proj: bfloat16 [1536, 1536], P(None, 'mp')
The draws below stay inside these ranges and needn't reach their ends.
All inputs are finite; a program needn't handle non-finite values.
Results may differ from the reference program's by a relative error of at most 0.012.
Values may be sent and summed in bfloat16 or wider, within the bound.
A program may use at most 64 MiB of HBM per device.

```python
import math
import jax
import jax.numpy as jnp
from jax import lax

D = 1536
HEADS = 16
HEAD_DIM = 96
SLICES = 8
LENGTH = 2560


def row_spread(key):
    return jnp.exp(jax.random.uniform(key, (SLICES, LENGTH, HEADS, 1), minval=math.log(0.3), maxval=math.log(3.0)))


def drawn_rows(key):
    values = jax.random.truncated_normal(jax.random.fold_in(key, 2), -2.6, 2.6, (SLICES, LENGTH, HEADS, HEAD_DIM))
    return values * row_spread(jax.random.fold_in(key, 1))


def draw_query(key, part):
    key = jax.random.fold_in(key, 7)
    values = drawn_rows(key)
    return values.reshape(SLICES, LENGTH, D).astype(jnp.bfloat16)


def draw_key(key, part):
    key = jax.random.fold_in(key, 9)
    values = drawn_rows(key)
    return values.reshape(SLICES, LENGTH, D).astype(jnp.bfloat16)


def levels(stream_key, dims, pieces, smallest, top_value):
    level = 1.0
    for dim, parts in pieces:
        heights = jax.random.uniform(jax.random.fold_in(jax.random.fold_in(stream_key, 6), dim), (parts,), jnp.float32, smallest / len(pieces), top_value / len(pieces))
        level = level * jnp.repeat(jnp.exp(heights), dims[dim] // parts).reshape((-1,) + (1,) * (len(dims) - 1 - dim))
    return level


def bell_draw(key, shape, scale, most, cuts=(), dtype=jnp.bfloat16):
    result = jax.random.normal(key, shape, jnp.float32) * scale
    if len(cuts) > 0:
        result = levels(key, shape, cuts, -0.22, 0.18) * result
    return jnp.clip(result, min=-most, max=most).astype(dtype)


def setup_inputs(seed: int = 0) -> dict:
    seeds = jax.random.split(jax.random.key(seed), 6)
    query = draw_query(jax.random.fold_in(seeds[5], 71), 0)
    key = draw_key(jax.random.fold_in(seeds[5], 71), 0)
    value = bell_draw(seeds[2], (SLICES, LENGTH, D), 1.0, 6.0, ((0, 8), (1, 16)))
    proj_weight = bell_draw(seeds[3], (D, D), D ** -0.5, 0.15625, ((1, 4),))
    grad_out = bell_draw(seeds[4], (SLICES, LENGTH, D), 1.0, 6.0, ((0, 8), (1, 16), (2, 4)))
    return dict(query=query, key=key, value=value, proj_weight=proj_weight, grad_out=grad_out)


def head_softmax(query_head, key_head):
    scores = jnp.dot(query_head, key_head.T, preferred_element_type=jnp.float32) * (1.0 / math.sqrt(HEAD_DIM))
    row_top = lax.optimization_barrier(jnp.max(scores, axis=1, keepdims=True))
    unscaled = jnp.exp(scores - row_top)
    row_total = lax.optimization_barrier(jnp.sum(unscaled, axis=1, keepdims=True))
    return (unscaled, row_total)

def forward_head(operands):
    query_head, key_head, value_head = operands
    unscaled, row_total = head_softmax(query_head, key_head)
    weights = unscaled.astype(jnp.bfloat16)
    summed = jnp.dot(weights, value_head, preferred_element_type=jnp.float32)
    return summed / row_total

def backward_head(operands):
    query_head, key_head, value_head, context_wide, grad_head = operands
    unscaled, row_total = head_softmax(query_head, key_head)
    probabilities = unscaled / row_total
    grad_probs = jnp.dot(grad_head, value_head.T, preferred_element_type=jnp.float32)
    row_delta = lax.optimization_barrier(jnp.sum(grad_head.astype(jnp.float32) * context_wide, axis=1, keepdims=True))
    grad_scores = (probabilities * (grad_probs - row_delta) * (1.0 / math.sqrt(HEAD_DIM))).astype(jnp.bfloat16)
    query_grads = jnp.dot(grad_scores, key_head, preferred_element_type=jnp.float32).astype(jnp.bfloat16)
    key_grads = jnp.dot(grad_scores.T, query_head, preferred_element_type=jnp.float32).astype(jnp.bfloat16)
    back_weights = probabilities.astype(jnp.bfloat16)
    value_grads = jnp.dot(back_weights.T, grad_head, preferred_element_type=jnp.float32).astype(jnp.bfloat16)
    return (query_grads, key_grads, value_grads)

def split_heads(array):
    return array.reshape(LENGTH, HEADS, HEAD_DIM).transpose(1, 0, 2)

def join_heads(array):
    return array.transpose(1, 0, 2).reshape(LENGTH, D)

def reference(query, key, value, proj_weight, grad_out):
    attended_list = []
    query_list = []
    key_list = []
    value_list = []
    grad_total = jnp.zeros((D, D), jnp.float32)
    for member in range(SLICES):
        heads_query = split_heads(query[member])
        heads_key = split_heads(key[member])
        heads_value = split_heads(value[member])
        context_wide = lax.map(forward_head, (heads_query, heads_key, heads_value))
        context = join_heads(context_wide.astype(jnp.bfloat16))
        attended_list.append(jnp.dot(context, proj_weight, preferred_element_type=jnp.float32).astype(jnp.bfloat16))
        grad_total = grad_total + jnp.dot(context.T, grad_out[member], preferred_element_type=jnp.float32)
        grad_context = jnp.dot(grad_out[member], proj_weight.T, preferred_element_type=jnp.float32).astype(jnp.bfloat16)
        query_grads, key_grads, value_grads = lax.map(backward_head, (heads_query, heads_key, heads_value, context_wide, split_heads(grad_context)))
        query_list.append(join_heads(query_grads))
        key_list.append(join_heads(key_grads))
        value_list.append(join_heads(value_grads))
    return (jnp.stack(attended_list), jnp.stack(query_list), jnp.stack(key_list), jnp.stack(value_list), grad_total.astype(jnp.bfloat16))
```

```python
import math

import jax
import jax.numpy as jnp
from jax import lax
from jax.experimental import pallas as pl
from jax.experimental.pallas import tpu as pltpu
from jax.sharding import PartitionSpec as P

MESH = pl.DeviceIdType.MESH
F32 = jnp.float32
BF16 = jnp.bfloat16
HD = 96
SCALE = 1.0 / math.sqrt(HD)
EXP2_SCALE = SCALE * math.log2(math.e)
NT = (((1,), (1,)), ((), ()))
NN = (((1,), (0,)), ((), ()))
TN = (((0,), (0,)), ((), ()))
FR = 160
QN = 640
CW = 384


def dot(a, b, dims):
    return lax.dot_general(a, b, dims, preferred_element_type=F32)


def copy_to(src, dst, send, recv, device):
    return pltpu.make_async_remote_copy(
        src_ref=src, dst_ref=dst, send_sem=send, recv_sem=recv, device_id=device, device_id_type=MESH
    )


def kernel(
    q_ref, k_ref, v_ref, w_ref, go_ref,
    att_ref, gq_ref, gk_ref, gv_ref, gp_ref,
    zsq, zskv, qbuf, kvbuf, gcs, gcr, gall, scores, ctxt, ctxs, ctxr, dqt, dqf, rss, rsr, own_kv,
    gqs, gqr, gks, gkr, att_acc, gps, gpr, gpo, gsum, xst, xrt, zst, gpf,
    zq_s, zq_r, zkv_s, zkv_r, xkv_s, xkv_r, gc_s, gc_r, ctx_s, ctx_r, rs_s, rs_r,
    gq_s, gq_r, gk_s, gk_r, gp_s, gp_r, px_s, px_r, pz_s, pz_r, ax_s, ax_r, ad_s, ad_r,
):
    d = lax.axis_index("dp")
    s = lax.axis_index("seq")
    m = lax.axis_index("mp")
    x = s // 4
    zl = s % 4
    z = m * 4 + zl
    core = d % 2

    def zdev(zz):
        return {"seq": x * 4 + zz % 4, "mp": zz // 4}

    def xdev(xx):
        return {"seq": xx * 4 + zl}

    def ddev(dd):
        return {"dp": dd}

    barrier = pltpu.get_barrier_semaphore()
    for k in range(1, 16):
        pl.semaphore_signal(barrier, inc=1, device_id=zdev((z + k) % 16), device_id_type=MESH)
    for k in range(1, 4):
        pl.semaphore_signal(barrier, inc=1, device_id=xdev((x + k) % 4), device_id_type=MESH)
    for k in range(1, 8):
        pl.semaphore_signal(barrier, inc=1, device_id=ddev((d + k) % 8), device_id_type=MESH)

    def offset(j):
        return (0, 1, 2 - 4 * core, -1)[j]

    def head_of(j):
        return (z + offset(j) + 16) % 16

    rows = lax.broadcasted_iota(jnp.int32, (CW, HD), 0)
    cols = lax.broadcasted_iota(jnp.int32, (CW, HD), 1)
    for j in (1, 3, 2, 0):
        h = head_of(j)
        pick = jnp.where(rows - cols == HD * (h % 4), 1.0, 0.0).astype(BF16)
        window = pl.ds(pl.multiple_of(CW * (h // 4), 128), CW)
        kh = dot(k_ref[:, window], pick, NN).astype(BF16)
        vh = dot(v_ref[:, window], pick, NN).astype(BF16)
        qh = dot(q_ref[:, window], pick, NN).astype(BF16)
        if j == 0:
            kvbuf[0, 0] = kh
            kvbuf[0, 1] = vh
            qbuf[0:FR, :] = qh
        else:
            zskv[j, 0] = kh
            zskv[j, 1] = vh
            zsq[j] = qh

    pl.semaphore_wait(barrier, 25)

    def zkv_copy(j):
        return copy_to(zskv.at[j], kvbuf.at[j], zkv_s.at[j], zkv_r.at[j], zdev(head_of(j)))

    def zq_copy(j):
        return copy_to(zsq.at[j], qbuf.at[pl.ds(FR * j, FR)], zq_s.at[j], zq_r.at[j], zdev(head_of(j)))

    def xkv_copy(xo, j):
        slot = xo * 4 + j
        return copy_to(kvbuf.at[j], kvbuf.at[slot], xkv_s.at[slot], xkv_r.at[slot], xdev((x + xo) % 4))

    for j in (1, 3, 2):
        zkv_copy(j).start()
    for xo in (2, 1, 3):
        xkv_copy(xo, 0).start()
    for j in (1, 3, 2):
        zq_copy(j).start()

    def gc_copy(k):
        return copy_to(gcs.at[k], gcr.at[k], gc_s.at[k], gc_r.at[k], zdev((z + k) % 16))

    def gc_step(k):
        h = (z + k) % 16
        part = dot(go_ref[...], w_ref[pl.ds(pl.multiple_of(HD * h, 32), HD), :], NT)
        gcs[k] = part.astype(BF16)
        gc_copy(k).start()

    def forward_x(j):
        zkv_copy(j).wait_recv()
        for xo in (2, 1, 3):
            xkv_copy(xo, j).start()

    order = (8, 7, 9, 6, 10, 5, 11, 4, 12, 3, 13, 2, 14, 1, 15)
    for k in order[:5]:
        gc_step(k)
    forward_x(1)
    forward_x(3)
    for k in order[5:10]:
        gc_step(k)
    forward_x(2)
    for k in order[10:]:
        gc_step(k)
    gcs[0] = dot(go_ref[...], w_ref[pl.ds(pl.multiple_of(HD * z, 32), HD), :], NT).astype(BF16)

    for j in (1, 3, 2):
        zq_copy(j).wait_recv()

    def score_slot(slot, top):
        block = dot(kvbuf[slot, 0], qbuf[...], NT)
        scores[slot] = block
        return jnp.maximum(top, jnp.max(block.reshape(FR // 8, 8, QN), axis=0))

    top = jnp.full((8, QN), -jnp.inf, F32)
    top = lax.fori_loop(0, 4, score_slot, top)
    for xo in (1, 3, 2):
        for j in (0, 1, 3, 2):
            xkv_copy(xo, j).wait_recv()
            top = score_slot(xo * 4 + j, top)
    row_top = jnp.max(top, axis=0, keepdims=True)

    ctxt[...] = jnp.zeros_like(ctxt)

    def soft_slot(slot, total):
        p = jnp.exp2((scores[slot] - row_top) * EXP2_SCALE)
        scores[slot] = p
        ctxt[...] += dot(kvbuf[slot, 1], p.astype(BF16), TN)
        return total + jnp.sum(p.reshape(FR // 8, 8, QN), axis=0)

    total = lax.fori_loop(0, 16, soft_slot, jnp.zeros((8, QN), F32))
    inverse = 1.0 / jnp.sum(total, axis=0, keepdims=True)
    wide = ctxt[...] * inverse
    ctxt[...] = wide
    narrow = wide.T.astype(BF16)
    for j in range(4):
        ctxs[j] = narrow[j * FR : (j + 1) * FR, :]

    def ctx_copy(k):
        return copy_to(ctxs.at[k % 4], ctxr.at[k], ctx_s.at[k], ctx_r.at[k], zdev((z - k + 16) % 16))

    for k in order:
        ctx_copy(k).start()
    ctxr[0] = ctxs[0]

    for j in range(4):
        acc = None
        for i in range(4):
            k = j + 4 * i
            if k == 0:
                part = gcs[0]
            else:
                gc_copy(k).wait_recv()
                part = gcr[k]
            part = part.astype(F32)
            acc = part if acc is None else acc + part
        gall[j * FR : (j + 1) * FR, :] = acc.astype(BF16)
    delta = jnp.sum(gall[...].astype(F32).T * ctxt[...], axis=0, keepdims=True)

    dqt[...] = jnp.zeros_like(dqt)

    def back_slot(slot):
        p = scores[slot] * inverse
        gprob = dot(kvbuf[slot, 1], gall[...], NT)
        ds = (p * (gprob - delta) * SCALE).astype(BF16)
        dk = dot(ds, qbuf[...], NN)
        dv = dot(p.astype(BF16), gall[...], NN)
        dqt[...] += dot(kvbuf[slot, 0], ds, TN)
        return dk, dv

    def rs_copy(slot):
        xo = slot // 4
        return copy_to(rss.at[slot], rsr.at[slot], rs_s.at[slot], rs_r.at[slot], xdev((x - xo + 4) % 4))

    def away_slot(i, carry):
        slot = 15 - i
        dk, dv = back_slot(slot)
        rss[slot, 0] = dk.astype(BF16)
        rss[slot, 1] = dv.astype(BF16)
        rs_copy(slot).start()
        return carry

    lax.fori_loop(0, 12, away_slot, 0)

    def own_slot(slot, carry):
        dk, dv = back_slot(slot)
        own_kv[slot, 0] = dk
        own_kv[slot, 1] = dv
        return carry

    lax.fori_loop(0, 4, own_slot, 0)

    dqf[...] = dqt[...].T

    def gq_copy(k):
        return copy_to(gqs.at[k], gqr.at[k], gq_s.at[k], gq_r.at[k], zdev((z - k + 16) % 16))

    def gk_copy(k):
        return copy_to(gks.at[k], gkr.at[k], gk_s.at[k], gk_r.at[k], zdev((z - k + 16) % 16))

    def piece_start(k):
        return pl.multiple_of(40 * (((z - k + 16) % 16) // 4), 8)

    pad = jnp.zeros((8, HD), F32)
    for k in order:
        part = dqf[pl.ds(FR * (k % 4) + piece_start(k), 40), :]
        gqs[k] = jnp.concatenate([part, pad], axis=0).astype(BF16)
        gq_copy(k).start()
    gqr[0] = jnp.concatenate([dqf[pl.ds(piece_start(0), 40), :], pad], axis=0).astype(BF16)

    for j in range(4):
        for xo in (3, 2, 1):
            rs_copy(xo * 4 + j).wait_recv()
        for t in range(2):
            own_kv[j, t] = (
                own_kv[j, t]
                + rsr[4 + j, t].astype(F32)
                + rsr[8 + j, t].astype(F32)
                + rsr[12 + j, t].astype(F32)
            )

    def gk_piece(k):
        start = piece_start(k)
        return jnp.concatenate(
            [own_kv[k % 4, 0, pl.ds(start, 40), :], own_kv[k % 4, 1, pl.ds(start, 40), :]], axis=0
        ).astype(BF16)

    for k in order:
        gks[k] = gk_piece(k)
        gk_copy(k).start()
    gkr[0] = gk_piece(0)

    att_acc[...] = jnp.zeros_like(att_acc)

    def owner(k):
        h = (z + k) % 16
        return h // 2, h % 2

    def gp_copy(k):
        dd, hh = owner(k)
        e = (dd - d + 8) % 8
        return copy_to(gps.at[k], gpr.at[e, hh], gp_s.at[k], gp_r.at[e, hh], ddev(dd))

    for k in (0,) + order[::-1]:
        if k > 0:
            ctx_copy(k).wait_recv()
        h = (z + k) % 16
        dd, hh = owner(k)
        att_acc[...] += dot(ctxr[k], w_ref[pl.ds(pl.multiple_of(HD * h, 32), HD), :], NN)
        part = dot(ctxr[k], go_ref[...], TN)

        @pl.when(dd == d)
        def _():
            gpo[hh] = part

        @pl.when(dd != d)
        def _():
            gps[k] = part.astype(BF16)
            gp_copy(k).start()

    att_ref[...] = att_acc[...].astype(BF16)

    for hh in range(2):
        for e in range(1, 8):
            copy_to(gps.at[0], gpr.at[e, hh], gp_s.at[0], gp_r.at[e, hh], ddev((d + e) % 8)).wait_recv()
        acc = gpo[hh]
        for e in range(1, 8):
            acc = acc + gpr[e, hh].astype(F32)
        gsum[hh] = acc

    def px_copy(xo):
        return copy_to(xst.at[xo], xrt.at[xo], px_s.at[xo], px_r.at[xo], xdev((x + xo) % 4))

    def quarter(xx):
        return gsum[xx // 2, pl.ds(pl.multiple_of(48 * (xx % 2), 16), 48), :]

    for xo in (2, 1, 3):
        xst[xo] = quarter((x + xo) % 4).astype(BF16)
        px_copy(xo).start()
    acc = quarter(x)
    for xo in (1, 3, 2):
        px_copy(xo).wait_recv()
        acc = acc + xrt[xo].astype(F32)
    zst[zl] = acc.astype(BF16)

    def pz_copy(o, source):
        return copy_to(
            zst.at[zl], zst.at[source], pz_s.at[o], pz_r.at[o], {"seq": x * 4 + (zl + o) % 4}
        )

    for o in (2, 1, 3):
        pz_copy(o, zl).start()
    for o in (1, 3, 2):
        pz_copy(o, (zl - o + 4) % 4).wait_recv()
    acc = zst[0].astype(F32)
    for i in range(1, 4):
        acc = acc + zst[i].astype(F32)
    gpf[d, x] = acc.astype(BF16)

    def ax_copy(xo, source):
        return copy_to(gpf.at[d, x], gpf.at[d, source], ax_s.at[xo], ax_r.at[xo], xdev((x + xo) % 4))

    def ad_copy(e, source):
        return copy_to(gpf.at[d], gpf.at[source], ad_s.at[e], ad_r.at[e], ddev((d + e) % 8))

    for xo in (2, 1, 3):
        ax_copy(xo, x).start()
    for xo in (1, 3, 2):
        ax_copy(xo, (x - xo + 4) % 4).wait_recv()
    for e in range(1, 8):
        ad_copy(e, d).start()

    for k in order:
        gq_copy(k).wait_recv()
        gk_copy(k).wait_recv()
    for group in range(4):
        lanes = pl.ds(CW * group, CW)
        slots = [(4 * group + i - z + 16) % 16 for i in range(4)]
        gq_ref[:, lanes] = jnp.concatenate([gqr[t, 0:40, :] for t in slots], axis=1)
        gk_ref[:, lanes] = jnp.concatenate([gkr[t, 0:40, :] for t in slots], axis=1)
        gv_ref[:, lanes] = jnp.concatenate([gkr[t, 40:80, :] for t in slots], axis=1)

    for e in range(1, 8):
        ad_copy(e, (d - e + 8) % 8).wait_recv()
    for i in range(8):
        for t in range(4):
            gp_ref[192 * i + 48 * t : 192 * i + 48 * (t + 1), :] = gpf[i, t]

    for j in range(1, 4):
        zkv_copy(j).wait_send()
        zq_copy(j).wait_send()
        px_copy(j).wait_send()
        pz_copy(j, zl).wait_send()
        ax_copy(j, x).wait_send()
    for xo in range(1, 4):
        for j in range(4):
            xkv_copy(xo, j).wait_send()
            rs_copy(xo * 4 + j).wait_send()
    for k in range(1, 16):
        gc_copy(k).wait_send()
        ctx_copy(k).wait_send()
        gq_copy(k).wait_send()
        gk_copy(k).wait_send()
    for k in range(16):

        @pl.when(owner(k)[0] != d)
        def _():
            gp_copy(k).wait_send()

    for e in range(1, 8):
        ad_copy(e, d).wait_send()


def per_device(query, key, value, proj_weight, grad_out):
    vmem = pl.BlockSpec(memory_space=pltpu.VMEM)
    dma = pltpu.SemaphoreType.DMA
    width = query.shape[2]
    outs = pl.pallas_call(
        kernel,
        out_shape=(
            jax.ShapeDtypeStruct((FR, CW), BF16),
            jax.ShapeDtypeStruct((40, width), BF16),
            jax.ShapeDtypeStruct((40, width), BF16),
            jax.ShapeDtypeStruct((40, width), BF16),
            jax.ShapeDtypeStruct((width, CW), BF16),
        ),
        in_specs=[vmem] * 5,
        out_specs=(vmem,) * 5,
        scratch_shapes=[
            pltpu.VMEM((4, FR, HD), BF16),
            pltpu.VMEM((4, 2, FR, HD), BF16),
            pltpu.VMEM((QN, HD), BF16),
            pltpu.VMEM((16, 2, FR, HD), BF16),
            pltpu.VMEM((16, FR, HD), BF16),
            pltpu.VMEM((16, FR, HD), BF16),
            pltpu.VMEM((QN, HD), BF16),
            pltpu.VMEM((16, FR, QN), F32),
            pltpu.VMEM((HD, QN), F32),
            pltpu.VMEM((4, FR, HD), BF16),
            pltpu.VMEM((16, FR, HD), BF16),
            pltpu.VMEM((HD, QN), F32),
            pltpu.VMEM((QN, HD), F32),
            pltpu.VMEM((16, 2, FR, HD), BF16),
            pltpu.VMEM((16, 2, FR, HD), BF16),
            pltpu.VMEM((4, 2, FR, HD), F32),
            pltpu.VMEM((16, 48, HD), BF16),
            pltpu.VMEM((16, 48, HD), BF16),
            pltpu.VMEM((16, 80, HD), BF16),
            pltpu.VMEM((16, 80, HD), BF16),
            pltpu.VMEM((FR, CW), F32),
            pltpu.VMEM((16, HD, CW), BF16),
            pltpu.VMEM((8, 2, HD, CW), BF16),
            pltpu.VMEM((2, HD, CW), F32),
            pltpu.VMEM((2, HD, CW), F32),
            pltpu.VMEM((4, 48, CW), BF16),
            pltpu.VMEM((4, 48, CW), BF16),
            pltpu.VMEM((4, 48, CW), BF16),
            pltpu.VMEM((8, 4, 48, CW), BF16),
            dma((4,)), dma((4,)),
            dma((4,)), dma((4,)),
            dma((16,)), dma((16,)),
            dma((16,)), dma((16,)),
            dma((16,)), dma((16,)),
            dma((16,)), dma((16,)),
            dma((16,)), dma((16,)),
            dma((16,)), dma((16,)),
            dma((16,)), dma((8, 2)),
            dma((4,)), dma((4,)),
            dma((4,)), dma((4,)),
            dma((4,)), dma((4,)),
            dma((8,)), dma((8,)),
        ],
        compiler_params=pltpu.CompilerParams(
            collective_id=0, has_side_effects=True, vmem_limit_bytes=48 * 1024 * 1024
        ),
        name="attention",
    )(query[0], key[0], value[0], proj_weight, grad_out[0])
    att, gq, gk, gv, gp = outs
    return att[None], gq[None], gk[None], gv[None], gp


def solution(mesh):
    return jax.shard_map(
        per_device,
        mesh=mesh,
        in_specs=(
            P("dp", "seq", None),
            P("dp", "seq", None),
            P("dp", "seq", None),
            P(None, "mp"),
            P("dp", "seq", "mp"),
        ),
        out_specs=(
            P("dp", "seq", "mp"),
            P("dp", ("seq", "mp"), None),
            P("dp", ("seq", "mp"), None),
            P("dp", ("seq", "mp"), None),
            P(None, "mp"),
        ),
        check_vma=False,
    )
```

```python
import math

import jax
import jax.numpy as jnp
from jax import lax
from jax.experimental import pallas as pl
from jax.experimental.pallas import tpu as pltpu
from jax.sharding import PartitionSpec as P

MESH = pl.DeviceIdType.MESH
F32 = jnp.float32
BF16 = jnp.bfloat16
HD = 96
SCALE = 1.0 / math.sqrt(HD)
EXP2_SCALE = SCALE * math.log2(math.e)
NT = (((1,), (1,)), ((), ()))
NN = (((1,), (0,)), ((), ()))
TN = (((0,), (0,)), ((), ()))
FR = 160
QN = 640
CW = 384


def dot(a, b, dims):
    return lax.dot_general(a, b, dims, preferred_element_type=F32)


def pack(block):
    t = block.shape[0] // 5
    tail = block[4 * t :, :]
    side = jnp.concatenate(
        [tail[:, 0:32], tail[:, 32:64], tail[:, 64:96], jnp.zeros((t, 32), block.dtype)], axis=0
    )
    return jnp.concatenate([block[: 4 * t, :], side], axis=1)


def unpack(block):
    t = block.shape[0] // 4
    side = block[:, 96:128]
    tail = jnp.concatenate([side[0:t], side[t : 2 * t], side[2 * t : 3 * t]], axis=1)
    return jnp.concatenate([block[:, 0:96], tail], axis=0)


def pack_pair(a, b):
    low = jnp.concatenate([b[0:80, 32:96], b[80:160, 32:96]], axis=1)
    return jnp.concatenate([jnp.concatenate([a, b[:, 0:32]], axis=1), low], axis=0)


def unpack_pair(block):
    low = jnp.concatenate([block[160:240, 0:64], block[160:240, 64:128]], axis=0)
    return block[0:160, 0:96], jnp.concatenate([block[0:160, 96:128], low], axis=1)


def copy_to(src, dst, send, recv, device):
    return pltpu.make_async_remote_copy(
        src_ref=src, dst_ref=dst, send_sem=send, recv_sem=recv, device_id=device, device_id_type=MESH
    )


def kernel(
    q_hbm, k_hbm, v_hbm, w_hbm, go_hbm,
    att_ref, gq_ref, gk_ref, gv_ref, gp_ref,
    q_ref, k_ref, v_ref, w_ref, go_ref,
    zsq, zskv, qin, qbuf, kvbuf, vbuf, gcs, gcr, gall, scores, tops, ctxt, ctxs, ctxr, dqt, dqf, rss, rsr, own_kv, gk_all, gv_all,
    gqs, gqr, gks, gkr, att_acc, gps, gpr, gpo, gsum, gsb, prr, gpf,
    zq_s, zq_r, zkv_s, zkv_r, xkv_s, xkv_r, gc_s, gc_r, ctx_s, ctx_r, rs_s, rs_r,
    gq_s, gq_r, gk_s, gk_r, gp_s, gp_r, ps_s, ps_r, as_s, as_r, ad_s, ad_r, ac_s, ac_r, in_s,
):
    d = lax.axis_index("dp")
    s = lax.axis_index("seq")
    m = lax.axis_index("mp")
    x = s // 4
    zl = s % 4
    z = m * 4 + zl
    core = d % 2

    def zdev(zz):
        return {"seq": x * 4 + zz % 4, "mp": zz // 4}

    def xdev(xx):
        return {"seq": xx * 4 + zl}

    def ddev(dd):
        return {"dp": dd}

    barrier = pltpu.get_barrier_semaphore()
    for k in range(1, 16):
        pl.semaphore_signal(barrier, inc=1, device_id=zdev((z + k) % 16), device_id_type=MESH)
    for k in range(1, 4):
        for i in range(4):
            row = {"seq": (x + k) % 4 * 4 + (zl + i) % 4}
            pl.semaphore_signal(barrier, inc=1, device_id=row, device_id_type=MESH)
    for k in range(1, 8):
        pl.semaphore_signal(barrier, inc=1, device_id=ddev((d + k) % 8), device_id_type=MESH)

    fetches = [
        pltpu.make_async_copy(src, dst, in_s.at[i])
        for i, (src, dst) in enumerate(
            ((k_hbm, k_ref), (v_hbm, v_ref), (q_hbm, q_ref), (w_hbm, w_ref), (go_hbm, go_ref))
        )
    ]
    for fetch in fetches:
        fetch.start()

    def offset(j):
        return (0, 1, 2 - 4 * core, -1)[j]

    def head_of(j):
        return (z + offset(j) + 16) % 16

    rows = lax.broadcasted_iota(jnp.int32, (CW, HD), 0)
    cols = lax.broadcasted_iota(jnp.int32, (CW, HD), 1)
    wide_rows = lax.broadcasted_iota(jnp.int32, (CW, 128), 0)
    wide_cols = lax.broadcasted_iota(jnp.int32, (CW, 128), 1)

    def wide_pick(start, lane, count):
        inside = (wide_cols >= lane) & (wide_cols < lane + count)
        return jnp.where((wide_rows - start == wide_cols - lane) & inside, 1.0, 0.0).astype(BF16)

    def window(h):
        return pl.ds(pl.multiple_of(CW * (h // 4), 128), CW)

    fetches[0].wait()
    fetches[1].wait()
    for j in (1, 3, 2, 0):
        h = head_of(j)
        start = HD * (h % 4)
        kh = k_ref[:, window(h)]
        vh = v_ref[:, window(h)]
        top_part = dot(kh, wide_pick(start, 0, 96), NN) + dot(vh, wide_pick(start, 96, 32), NN)
        low_part = dot(vh[0:80], wide_pick(start + 32, 0, 64), NN) + dot(
            vh[80:160], wide_pick(start + 32, 64, 64), NN
        )
        if j == 0:
            kvbuf[0, 0:160, :] = top_part.astype(BF16)
            kvbuf[0, 160:240, :] = low_part.astype(BF16)
        else:
            zskv[j, 0:160, :] = top_part.astype(BF16)
            zskv[j, 160:240, :] = low_part.astype(BF16)

    pl.semaphore_wait(barrier, 34)

    def zkv_copy(j):
        return copy_to(zskv.at[j], kvbuf.at[j], zkv_s.at[j], zkv_r.at[j], zdev(head_of(j)))

    def zq_copy(j):
        return copy_to(zsq.at[j], qin.at[j], zq_s.at[j], zq_r.at[j], zdev(head_of(j)))

    def xkv_copy(xo, j):
        slot = xo * 4 + j
        return copy_to(kvbuf.at[j], kvbuf.at[slot], xkv_s.at[slot], xkv_r.at[slot], xdev((x + xo) % 4))

    for j in (1, 3, 2):
        zkv_copy(j).start()
    for xo in (2, 1, 3):
        xkv_copy(xo, 0).start()
    fetches[2].wait()
    for j in (1, 3, 2, 0):
        h = head_of(j)
        pick = jnp.where(rows - cols == HD * (h % 4), 1.0, 0.0).astype(BF16)
        qh = dot(q_ref[:, window(h)], pick, NN)
        if j == 0:
            qbuf[0:FR, :] = qh.astype(BF16)
        else:
            zsq[j] = pack(qh).astype(BF16)
            zq_copy(j).start()
    fetches[3].wait()
    fetches[4].wait()

    def gc_copy(k):
        return copy_to(gcs.at[k], gcr.at[k], gc_s.at[k], gc_r.at[k], zdev((z + k) % 16))

    def gc_step(k):
        h = (z + k) % 16
        part = dot(go_ref[...], w_ref[pl.ds(pl.multiple_of(HD * h, 32), HD), :], NT)
        gcs[k] = pack(part).astype(BF16)

    order = (8, 7, 9, 6, 10, 5, 11, 4, 12, 3, 13, 2, 14, 1, 15)
    for k in order:
        gc_step(k)
    for j in (1, 3, 2):
        zkv_copy(j).wait_recv()
        for xo in (2, 1, 3):
            xkv_copy(xo, j).start()
    for k in order:
        gc_copy(k).start()
    gcs[0] = pack(dot(go_ref[...], w_ref[pl.ds(pl.multiple_of(HD * z, 32), HD), :], NT)).astype(BF16)

    for j in (1, 3, 2):
        zq_copy(j).wait_recv()
        qbuf[FR * j : FR * (j + 1), :] = unpack(qin[j].astype(F32)).astype(BF16)

    ctxt[...] = jnp.zeros_like(ctxt)

    def score_slot(slot, carry):
        top, total = carry
        keys, values = unpack_pair(kvbuf[slot].astype(F32))
        values = values.astype(BF16)
        vbuf[slot] = values
        block = dot(keys.astype(BF16), qbuf[...], NT)
        new_top = jnp.maximum(top, jnp.max(block, axis=0, keepdims=True))
        keep = jnp.exp2((top - new_top) * EXP2_SCALE)
        p = jnp.exp2((block - new_top) * EXP2_SCALE)
        scores[slot] = p
        tops[slot] = new_top
        ctxt[...] = ctxt[...] * keep + dot(values, p.astype(BF16), TN)
        return new_top, total * keep + jnp.sum(p.reshape(FR // 8, 8, QN), axis=0)

    carry = (jnp.full((1, QN), -jnp.inf, F32), jnp.zeros((8, QN), F32))
    carry = lax.fori_loop(0, 4, score_slot, carry)
    for xo in (1, 3, 2):
        for j in (0, 1, 3, 2):
            xkv_copy(xo, j).wait_recv()
            carry = score_slot(xo * 4 + j, carry)
    row_top, total = carry
    inverse = 1.0 / jnp.sum(total, axis=0, keepdims=True)
    wide = ctxt[...] * inverse
    ctxt[...] = wide
    narrow = wide.T
    for j in range(4):
        ctxs[j] = pack(narrow[j * FR : (j + 1) * FR, :]).astype(BF16)

    def ctx_copy(k):
        return copy_to(ctxs.at[k % 4], ctxr.at[k], ctx_s.at[k], ctx_r.at[k], zdev((z - k + 16) % 16))

    for k in order:
        ctx_copy(k).start()
    ctxr[0] = ctxs[0]

    for j in range(4):
        acc = None
        for i in range(4):
            k = j + 4 * i
            if k == 0:
                part = gcs[0]
            else:
                gc_copy(k).wait_recv()
                part = gcr[k]
            part = part.astype(F32)
            acc = part if acc is None else acc + part
        gall[j * FR : (j + 1) * FR, :] = unpack(acc).astype(BF16)
    delta = jnp.sum(gall[...].astype(F32).T * ctxt[...], axis=0, keepdims=True)

    dqt[...] = jnp.zeros_like(dqt)

    def back_slot(slot):
        p = scores[slot] * (jnp.exp2((tops[slot] - row_top) * EXP2_SCALE) * inverse)
        gprob = dot(vbuf[slot], gall[...], NT)
        ds = (p * (gprob - delta) * SCALE).astype(BF16)
        dk = dot(ds, qbuf[...], NN)
        dv = dot(p.astype(BF16), gall[...], NN)
        dqt[...] += dot(kvbuf[slot, 0:160, 0:96], ds, TN)
        return pack_pair(dk, dv)

    def rs_copy(slot):
        xo = slot // 4
        return copy_to(rss.at[slot], rsr.at[slot], rs_s.at[slot], rs_r.at[slot], xdev((x - xo + 4) % 4))

    def away_slot(i, carry):
        slot = 15 - i
        rss[slot] = back_slot(slot).astype(BF16)
        rs_copy(slot).start()
        return carry

    lax.fori_loop(0, 12, away_slot, 0)

    def own_slot(slot, carry):
        own_kv[slot] = back_slot(slot)
        return carry

    lax.fori_loop(0, 4, own_slot, 0)

    dqf[...] = dqt[...].T

    def gq_copy(k):
        return copy_to(gqs.at[k], gqr.at[k], gq_s.at[k], gq_r.at[k], zdev((z - k + 16) % 16))

    def gk_copy(k):
        return copy_to(gks.at[k], gkr.at[k], gk_s.at[k], gk_r.at[k], zdev((z - k + 16) % 16))

    def piece_start(k):
        return pl.multiple_of(40 * (((z - k + 16) % 16) // 4), 8)

    def gq_piece(k):
        return pack(dqf[pl.ds(FR * (k % 4) + piece_start(k), 40), :]).astype(BF16)

    for k in order:
        gqs[k] = gq_piece(k)
        gq_copy(k).start()
    gqr[0] = gq_piece(0)

    for j in range(4):
        for xo in (3, 2, 1):
            rs_copy(xo * 4 + j).wait_recv()
        summed = (
            own_kv[j] + rsr[4 + j].astype(F32) + rsr[8 + j].astype(F32) + rsr[12 + j].astype(F32)
        )
        gk_all[j], gv_all[j] = unpack_pair(summed)

    def gk_piece(k):
        rows40 = pl.ds(piece_start(k), 40)
        return pack(
            jnp.concatenate([gk_all[k % 4, rows40, :], gv_all[k % 4, rows40, :]], axis=0)
        ).astype(BF16)

    for k in order:
        gks[k] = gk_piece(k)
        gk_copy(k).start()
    gkr[0] = gk_piece(0)


    att_acc[...] = jnp.zeros_like(att_acc)

    def owner(k):
        h = (z + k) % 16
        return h // 2, h % 2

    def gp_copy(k):
        dd, hh = owner(k)
        e = (dd - d + 8) % 8
        return copy_to(gps.at[k], gpr.at[e, hh], gp_s.at[k], gp_r.at[e, hh], ddev(dd))

    for k in (0,) + order[::-1]:
        if k > 0:
            ctx_copy(k).wait_recv()
        h = (z + k) % 16
        dd, hh = owner(k)
        context = unpack(ctxr[k].astype(F32)).astype(BF16)
        att_acc[...] += dot(context, w_ref[pl.ds(pl.multiple_of(HD * h, 32), HD), :], NN)
        part = dot(context, go_ref[...], TN)

        @pl.when(dd == d)
        def _():
            gpo[hh] = part

        @pl.when(dd != d)
        def _():
            gps[k] = part.astype(BF16)
            gp_copy(k).start()

    for hh in range(2):
        for e in range(1, 8):
            copy_to(gps.at[0], gpr.at[e, hh], gp_s.at[0], gp_r.at[e, hh], ddev((d + e) % 8)).wait_recv()
        acc = gpo[hh]
        for e in range(1, 8):
            acc = acc + gpr[e, hh].astype(F32)
        gsum[96 * hh : 96 * (hh + 1), :] = acc
        gsb[96 * hh : 96 * (hh + 1), :] = acc.astype(BF16)

    att_ref[...] = att_acc[...].astype(BF16)

    def share(i):
        return pl.ds(pl.multiple_of(16 * i, 16), 16)

    def ps_copy(o):
        i = (s + o) % 16
        return copy_to(gsb.at[share(i)], prr.at[o], ps_s.at[o], ps_r.at[o], {"seq": i})

    def as_copy(o, source):
        rows16 = gpf.at[d, share(source)]
        return copy_to(rows16, rows16, as_s.at[o], as_r.at[o], {"seq": (s + o) % 16})

    for o in range(1, 16):

        @pl.when((s + o) % 16 < 12)
        def _():
            ps_copy(o).start()

    @pl.when(s < 12)
    def _():
        acc = gsum[share(s), :]
        for o in range(1, 16):
            copy_to(gsb.at[0:16], prr.at[o], ps_s.at[o], ps_r.at[o], {"seq": (s + o) % 16}).wait_recv()
            acc = acc + prr[o].astype(F32)
        gpf[d, share(s), :] = acc.astype(BF16)
        for o in range(1, 16):
            as_copy(o, s).start()

    def ad_copy(e, source):
        return copy_to(gpf.at[d], gpf.at[source], ad_s.at[e], ad_r.at[e], ddev((d + 2 * e) % 8))

    def ac_copy(e, mine, other):
        return copy_to(gpf.at[mine], gpf.at[other], ac_s.at[e], ac_r.at[e], ddev(d + 1 - 2 * core))

    def ac_source(e):
        return (d - 2 * e + 8) % 8

    for o in range(1, 16):
        source = (s - o + 16) % 16

        @pl.when(source < 12)
        def _():
            as_copy(o, source).wait_recv()

    for e in (2, 1, 3):
        ad_copy(e, d).start()
    ac_copy(0, d, d).start()

    for k in order:
        gq_copy(k).wait_recv()
        gk_copy(k).wait_recv()

    for group in range(4):
        lanes = pl.ds(CW * group, CW)
        slots = [(4 * group + i - z + 16) % 16 for i in range(4)]
        queries = [unpack(gqr[t].astype(F32)) for t in slots]
        pairs = [unpack(gkr[t].astype(F32)) for t in slots]
        gq_ref[:, lanes] = jnp.concatenate(queries, axis=1).astype(BF16)
        gk_ref[:, lanes] = jnp.concatenate([p[0:40] for p in pairs], axis=1).astype(BF16)
        gv_ref[:, lanes] = jnp.concatenate([p[40:80] for p in pairs], axis=1).astype(BF16)

    for e in (1, 3, 2):
        ad_copy(e, ac_source(e)).wait_recv()
        ac_copy(e, ac_source(e), ac_source(e)).start()
    sibling = d + 1 - 2 * core
    for e in range(4):
        ac_copy(e, d, (sibling - 2 * e + 8) % 8).wait_recv()
    for i in range(8):
        gp_ref[192 * i : 192 * (i + 1), :] = gpf[i]

    for j in range(1, 4):
        zkv_copy(j).wait_send()
        zq_copy(j).wait_send()
    for xo in range(1, 4):
        for j in range(4):
            xkv_copy(xo, j).wait_send()
            rs_copy(xo * 4 + j).wait_send()
    for k in range(1, 16):
        gc_copy(k).wait_send()
        ctx_copy(k).wait_send()
        gq_copy(k).wait_send()
        gk_copy(k).wait_send()
    for k in range(16):

        @pl.when(owner(k)[0] != d)
        def _():
            gp_copy(k).wait_send()

    for o in range(1, 16):

        @pl.when((s + o) % 16 < 12)
        def _():
            ps_copy(o).wait_send()

    @pl.when(s < 12)
    def _():
        for o in range(1, 16):
            as_copy(o, s).wait_send()

    for e in range(1, 4):
        ad_copy(e, d).wait_send()
    for e in range(4):
        ac_copy(e, ac_source(e), ac_source(e)).wait_send()


def per_device(query, key, value, proj_weight, grad_out):
    vmem = pl.BlockSpec(memory_space=pltpu.VMEM)
    dma = pltpu.SemaphoreType.DMA
    width = query.shape[2]
    outs = pl.pallas_call(
        kernel,
        out_shape=(
            jax.ShapeDtypeStruct((FR, CW), BF16),
            jax.ShapeDtypeStruct((40, width), BF16),
            jax.ShapeDtypeStruct((40, width), BF16),
            jax.ShapeDtypeStruct((40, width), BF16),
            jax.ShapeDtypeStruct((width, CW), BF16),
        ),
        in_specs=[pl.BlockSpec(memory_space=pltpu.HBM)] * 5,
        out_specs=(vmem,) * 5,
        scratch_shapes=[
            pltpu.VMEM((FR, width), BF16),
            pltpu.VMEM((FR, width), BF16),
            pltpu.VMEM((FR, width), BF16),
            pltpu.VMEM((width, CW), BF16),
            pltpu.VMEM((FR, CW), BF16),
            pltpu.VMEM((4, 128, 128), BF16),
            pltpu.VMEM((4, 240, 128), BF16),
            pltpu.VMEM((4, 128, 128), BF16),
            pltpu.VMEM((QN, HD), BF16),
            pltpu.VMEM((16, 240, 128), BF16),
            pltpu.VMEM((16, FR, HD), BF16),
            pltpu.VMEM((16, 128, 128), BF16),
            pltpu.VMEM((16, 128, 128), BF16),
            pltpu.VMEM((QN, HD), BF16),
            pltpu.VMEM((16, FR, QN), F32),
            pltpu.VMEM((16, 1, QN), F32),
            pltpu.VMEM((HD, QN), F32),
            pltpu.VMEM((4, 128, 128), BF16),
            pltpu.VMEM((16, 128, 128), BF16),
            pltpu.VMEM((HD, QN), F32),
            pltpu.VMEM((QN, HD), F32),
            pltpu.VMEM((16, 240, 128), BF16),
            pltpu.VMEM((16, 240, 128), BF16),
            pltpu.VMEM((4, 240, 128), F32),
            pltpu.VMEM((4, FR, HD), F32),
            pltpu.VMEM((4, FR, HD), F32),
            pltpu.VMEM((16, 32, 128), BF16),
            pltpu.VMEM((16, 32, 128), BF16),
            pltpu.VMEM((16, 64, 128), BF16),
            pltpu.VMEM((16, 64, 128), BF16),
            pltpu.VMEM((FR, CW), F32),
            pltpu.VMEM((16, HD, CW), BF16),
            pltpu.VMEM((8, 2, HD, CW), BF16),
            pltpu.VMEM((2, HD, CW), F32),
            pltpu.VMEM((192, CW), F32),
            pltpu.VMEM((192, CW), BF16),
            pltpu.VMEM((16, 16, CW), BF16),
            pltpu.VMEM((8, 192, CW), BF16),
            dma((4,)), dma((4,)),
            dma((4,)), dma((4,)),
            dma((16,)), dma((16,)),
            dma((16,)), dma((16,)),
            dma((16,)), dma((16,)),
            dma((16,)), dma((16,)),
            dma((16,)), dma((16,)),
            dma((16,)), dma((16,)),
            dma((16,)), dma((8, 2)),
            dma((16,)), dma((16,)),
            dma((16,)), dma((16,)),
            dma((4,)), dma((4,)),
            dma((4,)), dma((4,)),
            dma((5,)),
        ],
        compiler_params=pltpu.CompilerParams(
            collective_id=0, has_side_effects=True, vmem_limit_bytes=64 * 1024 * 1024 - 65536
        ),
        name="attention",
    )(query[0], key[0], value[0], proj_weight, grad_out[0])
    att, gq, gk, gv, gp = outs
    return att[None], gq[None], gk[None], gv[None], gp


def solution(mesh):
    return jax.shard_map(
        per_device,
        mesh=mesh,
        in_specs=(
            P("dp", "seq", None),
            P("dp", "seq", None),
            P("dp", "seq", None),
            P(None, "mp"),
            P("dp", "seq", "mp"),
        ),
        out_specs=(
            P("dp", "seq", "mp"),
            P("dp", ("seq", "mp"), None),
            P("dp", ("seq", "mp"), None),
            P("dp", ("seq", "mp"), None),
            P(None, "mp"),
        ),
        check_vma=False,
    )
```

```python
import math

import jax
import jax.numpy as jnp
from jax import lax
from jax.experimental import pallas as pl
from jax.experimental.pallas import tpu as pltpu
from jax.sharding import PartitionSpec as P

MESH = pl.DeviceIdType.MESH
F32 = jnp.float32
BF16 = jnp.bfloat16
HD = 96
SCALE = 1.0 / math.sqrt(HD)
EXP2_SCALE = SCALE * math.log2(math.e)
NT = (((1,), (1,)), ((), ()))
NN = (((1,), (0,)), ((), ()))
TN = (((0,), (0,)), ((), ()))
FR = 160
QN = 640
CW = 384


def dot(a, b, dims):
    return lax.dot_general(a, b, dims, preferred_element_type=F32)


def pack(block):
    t = block.shape[0] // 5
    tail = block[4 * t :, :]
    side = jnp.concatenate(
        [tail[:, 0:32], tail[:, 32:64], tail[:, 64:96], jnp.zeros((t, 32), block.dtype)], axis=0
    )
    return jnp.concatenate([block[: 4 * t, :], side], axis=1)


def unpack(block):
    t = block.shape[0] // 4
    side = block[:, 96:128]
    tail = jnp.concatenate([side[0:t], side[t : 2 * t], side[2 * t : 3 * t]], axis=1)
    return jnp.concatenate([block[:, 0:96], tail], axis=0)


def pack_pair(a, b):
    low = jnp.concatenate([b[0:80, 32:96], b[80:160, 32:96]], axis=1)
    return jnp.concatenate([jnp.concatenate([a, b[:, 0:32]], axis=1), low], axis=0)


def unpack_pair(block):
    low = jnp.concatenate([block[160:240, 0:64], block[160:240, 64:128]], axis=0)
    return block[0:160, 0:96], jnp.concatenate([block[0:160, 96:128], low], axis=1)


def copy_to(src, dst, send, recv, device):
    return pltpu.make_async_remote_copy(
        src_ref=src, dst_ref=dst, send_sem=send, recv_sem=recv, device_id=device, device_id_type=MESH
    )


def kernel(
    q_hbm, k_hbm, v_hbm, w_hbm, go_hbm,
    att_ref, gq_ref, gk_ref, gv_ref, gp_ref,
    q_ref, k_ref, v_ref, w_ref, go_ref,
    zsq, zskv, qin, qbuf, kvbuf, vbuf, gcs, gcm, gcr, gall, scores, tops, ctxt, ctxs, ctxr, dqt, dqf, rss, rsr, own_kv, gk_all, gv_all,
    gqs, gqr, gks, gkr, att_acc, gps, gpr, gpo, gsum, gsb, prr, gpf,
    zq_s, zq_r, zkv_s, zkv_r, xkv_s, xkv_r, gc_s, gc_r, ctx_s, ctx_r, rs_s, rs_r,
    gq_s, gq_r, gk_s, gk_r, gp_s, gp_r, ps_s, ps_r, as_s, as_r, ad_s, ad_r, ac_s, ac_r, in_s,
):
    d = lax.axis_index("dp")
    s = lax.axis_index("seq")
    m = lax.axis_index("mp")
    x = s // 4
    zl = s % 4
    z = m * 4 + zl
    core = d % 2

    def zdev(zz):
        return {"seq": x * 4 + zz % 4, "mp": zz // 4}

    def xdev(xx):
        return {"seq": xx * 4 + zl}

    def ddev(dd):
        return {"dp": dd}

    barrier = pltpu.get_barrier_semaphore()
    for k in range(1, 16):
        pl.semaphore_signal(barrier, inc=1, device_id=zdev((z + k) % 16), device_id_type=MESH)
    for k in range(1, 4):
        for i in range(4):
            row = {"seq": (x + k) % 4 * 4 + (zl + i) % 4}
            pl.semaphore_signal(barrier, inc=1, device_id=row, device_id_type=MESH)
    for k in range(1, 8):
        pl.semaphore_signal(barrier, inc=1, device_id=ddev((d + k) % 8), device_id_type=MESH)

    fetches = [
        pltpu.make_async_copy(src, dst, in_s.at[i])
        for i, (src, dst) in enumerate(
            ((k_hbm, k_ref), (v_hbm, v_ref), (q_hbm, q_ref), (w_hbm, w_ref), (go_hbm, go_ref))
        )
    ]
    for fetch in fetches:
        fetch.start()

    def offset(j):
        return (0, 1, 2 - 4 * core, -1)[j]

    def head_of(j):
        return (z + offset(j) + 16) % 16

    rows = lax.broadcasted_iota(jnp.int32, (CW, HD), 0)
    cols = lax.broadcasted_iota(jnp.int32, (CW, HD), 1)
    wide_rows = lax.broadcasted_iota(jnp.int32, (CW, 128), 0)
    wide_cols = lax.broadcasted_iota(jnp.int32, (CW, 128), 1)

    def wide_pick(start, lane, count):
        inside = (wide_cols >= lane) & (wide_cols < lane + count)
        return jnp.where((wide_rows - start == wide_cols - lane) & inside, 1.0, 0.0).astype(BF16)

    def window(h):
        return pl.ds(pl.multiple_of(CW * (h // 4), 128), CW)

    fetches[0].wait()
    fetches[1].wait()
    for j in (1, 3, 2, 0):
        h = head_of(j)
        start = HD * (h % 4)
        kh = k_ref[:, window(h)]
        vh = v_ref[:, window(h)]
        top_part = dot(kh, wide_pick(start, 0, 96), NN) + dot(vh, wide_pick(start, 96, 32), NN)
        low_part = dot(vh[0:80], wide_pick(start + 32, 0, 64), NN) + dot(
            vh[80:160], wide_pick(start + 32, 64, 64), NN
        )
        if j == 0:
            kvbuf[0, 0:160, :] = top_part.astype(BF16)
            kvbuf[0, 160:240, :] = low_part.astype(BF16)
        else:
            zskv[j, 0:160, :] = top_part.astype(BF16)
            zskv[j, 160:240, :] = low_part.astype(BF16)

    pl.semaphore_wait(barrier, 34)

    def zkv_copy(j):
        return copy_to(zskv.at[j], kvbuf.at[j], zkv_s.at[j], zkv_r.at[j], zdev(head_of(j)))

    def zq_copy(j):
        return copy_to(zsq.at[j], qin.at[j], zq_s.at[j], zq_r.at[j], zdev(head_of(j)))

    def xkv_copy(xo, j):
        slot = xo * 4 + j
        return copy_to(kvbuf.at[j], kvbuf.at[slot], xkv_s.at[slot], xkv_r.at[slot], xdev((x + xo) % 4))

    for j in (1, 3, 2):
        zkv_copy(j).start()
    for xo in (2, 1, 3):
        xkv_copy(xo, 0).start()
    fetches[2].wait()
    for j in (1, 3, 2, 0):
        h = head_of(j)
        pick = jnp.where(rows - cols == HD * (h % 4), 1.0, 0.0).astype(BF16)
        qh = dot(q_ref[:, window(h)], pick, NN)
        if j == 0:
            qbuf[0:FR, :] = qh.astype(BF16)
        else:
            zsq[j] = pack(qh).astype(BF16)
            zq_copy(j).start()
    fetches[3].wait()
    fetches[4].wait()

    def gc_copy(k):
        if 5 <= k <= 11:
            step = 4 if k <= 8 else -4
            return copy_to(gcs.at[k], gcm.at[k], gc_s.at[k], gc_r.at[k], zdev((z + step + 16) % 16))
        return copy_to(gcs.at[k], gcr.at[k], gc_s.at[k], gc_r.at[k], zdev((z + k) % 16))

    def gc_relay():
        for k in (4, 3, 13, 2, 14, 1, 15):
            far = k + 4 if k < 8 else k - 4
            gc_copy(far).wait_recv()
            gcs[k] = (gcs[k].astype(F32) + gcm[far].astype(F32)).astype(BF16)
            gc_copy(k).start()

    def gc_step(k):
        h = (z + k) % 16
        part = dot(go_ref[...], w_ref[pl.ds(pl.multiple_of(HD * h, 32), HD), :], NT)
        gcs[k] = pack(part).astype(BF16)

    order = (8, 7, 9, 6, 10, 5, 11, 4, 12, 3, 13, 2, 14, 1, 15)
    for k in order[:5]:
        gc_step(k)
    for j in (1, 3, 2):
        zkv_copy(j).wait_recv()
        for xo in (2, 1, 3):
            xkv_copy(xo, j).start()
    for k in order[:5]:
        gc_copy(k).start()
    for k in order[5:]:
        gc_step(k)
        if 5 <= k <= 12:
            gc_copy(k).start()
    gcs[0] = pack(dot(go_ref[...], w_ref[pl.ds(pl.multiple_of(HD * z, 32), HD), :], NT)).astype(BF16)

    for j in (1, 3, 2):
        zq_copy(j).wait_recv()
        qbuf[FR * j : FR * (j + 1), :] = unpack(qin[j].astype(F32)).astype(BF16)

    ctxt[...] = jnp.zeros_like(ctxt)

    def score_slot(slot, carry):
        top, total = carry
        keys, values = unpack_pair(kvbuf[slot].astype(F32))
        values = values.astype(BF16)
        vbuf[slot] = values
        block = dot(keys.astype(BF16), qbuf[...], NT)
        new_top = jnp.maximum(top, jnp.max(block, axis=0, keepdims=True))
        keep = jnp.exp2((top - new_top) * EXP2_SCALE)
        p = jnp.exp2((block - new_top) * EXP2_SCALE)
        scores[slot] = p
        tops[slot] = new_top
        ctxt[...] = ctxt[...] * keep + dot(values, p.astype(BF16), TN)
        return new_top, total * keep + jnp.sum(p.reshape(FR // 8, 8, QN), axis=0)

    carry = (jnp.full((1, QN), -jnp.inf, F32), jnp.zeros((8, QN), F32))
    carry = lax.fori_loop(0, 4, score_slot, carry)
    for xo in (1, 3, 2):
        for j in (0, 1, 3, 2):
            xkv_copy(xo, j).wait_recv()
            carry = score_slot(xo * 4 + j, carry)
        if xo == 1:
            gc_relay()
    row_top, total = carry
    inverse = 1.0 / jnp.sum(total, axis=0, keepdims=True)
    wide = ctxt[...] * inverse
    ctxt[...] = wide
    narrow = wide.T
    for j in range(4):
        ctxs[j] = pack(narrow[j * FR : (j + 1) * FR, :]).astype(BF16)

    def ctx_copy(k):
        if 5 <= k <= 11:
            source, step = (ctxr.at[k - 4], -4) if k <= 8 else (ctxr.at[k + 4], 4)
        else:
            source, step = ctxs.at[k % 4], -k
        return copy_to(source, ctxr.at[k], ctx_s.at[k], ctx_r.at[k], zdev((z + step + 16) % 16))

    for k in (4, 12, 3, 13, 2, 14, 1, 15):
        ctx_copy(k).start()
    ctxr[0] = ctxs[0]

    for j in range(4):
        acc = gcs[0].astype(F32) if j == 0 else None
        for k in (4, 12) if j == 0 else (j, j + 12):
            gc_copy(k).wait_recv()
            part = gcr[k].astype(F32)
            acc = part if acc is None else acc + part
        gall[j * FR : (j + 1) * FR, :] = unpack(acc).astype(BF16)
    for k in (4, 3, 13, 2, 14, 1, 15):
        ctx_copy(k).wait_recv()
        ctx_copy(k + 4 if k < 8 else k - 4).start()
    delta = jnp.sum(gall[...].astype(F32).T * ctxt[...], axis=0, keepdims=True)

    att_acc[...] = jnp.zeros_like(att_acc)

    def owner(k):
        h = (z + k) % 16
        return h // 2, h % 2

    def gp_copy(k):
        dd, hh = owner(k)
        e = (dd - d + 8) % 8
        return copy_to(gps.at[k], gpr.at[e, hh], gp_s.at[k], gp_r.at[e, hh], ddev(dd))

    def project(k):
        if 5 <= k <= 12:
            ctx_copy(k).wait_recv()
        h = (z + k) % 16
        dd, hh = owner(k)
        context = unpack(ctxr[k].astype(F32)).astype(BF16)
        att_acc[...] += dot(context, w_ref[pl.ds(pl.multiple_of(HD * h, 32), HD), :], NN)
        part = dot(context, go_ref[...], TN)

        @pl.when(dd == d)
        def _():
            gpo[hh] = part

        @pl.when(dd != d)
        def _():
            gps[k] = part.astype(BF16)
            gp_copy(k).start()

    dqt[...] = jnp.zeros_like(dqt)

    def back_slot(slot):
        p = scores[slot] * (jnp.exp2((tops[slot] - row_top) * EXP2_SCALE) * inverse)
        gprob = dot(vbuf[slot], gall[...], NT)
        ds = (p * (gprob - delta) * SCALE).astype(BF16)
        dk = dot(ds, qbuf[...], NN)
        dv = dot(p.astype(BF16), gall[...], NN)
        dqt[...] += dot(kvbuf[slot, 0:160, 0:96], ds, TN)
        return pack_pair(dk, dv)

    def rs_copy(slot):
        xo = slot // 4
        return copy_to(rss.at[slot], rsr.at[slot], rs_s.at[slot], rs_r.at[slot], xdev((x - xo + 4) % 4))

    def away_slot(i, carry):
        slot = 15 - i
        rss[slot] = back_slot(slot).astype(BF16)
        rs_copy(slot).start()
        return carry

    lax.fori_loop(0, 12, away_slot, 0)
    project(0)
    for k in order[:8:-1]:
        project(k)

    def own_slot(slot, carry):
        own_kv[slot] = back_slot(slot)
        return carry

    lax.fori_loop(0, 4, own_slot, 0)

    dqf[...] = dqt[...].T

    def gq_copy(k):
        return copy_to(gqs.at[k], gqr.at[k], gq_s.at[k], gq_r.at[k], zdev((z - k + 16) % 16))

    def gk_copy(k):
        return copy_to(gks.at[k], gkr.at[k], gk_s.at[k], gk_r.at[k], zdev((z - k + 16) % 16))

    def piece_start(k):
        return pl.multiple_of(40 * (((z - k + 16) % 16) // 4), 8)

    def gq_piece(k):
        return pack(dqf[pl.ds(FR * (k % 4) + piece_start(k), 40), :]).astype(BF16)

    for k in order:
        gqs[k] = gq_piece(k)
        gq_copy(k).start()
    gqr[0] = gq_piece(0)

    for k in order[8:3:-1]:
        project(k)

    for j in range(4):
        for xo in (3, 2, 1):
            rs_copy(xo * 4 + j).wait_recv()
        summed = (
            own_kv[j] + rsr[4 + j].astype(F32) + rsr[8 + j].astype(F32) + rsr[12 + j].astype(F32)
        )
        gk_all[j], gv_all[j] = unpack_pair(summed)

    def gk_piece(k):
        rows40 = pl.ds(piece_start(k), 40)
        return pack(
            jnp.concatenate([gk_all[k % 4, rows40, :], gv_all[k % 4, rows40, :]], axis=0)
        ).astype(BF16)

    for k in order:
        gks[k] = gk_piece(k)
        gk_copy(k).start()
    gkr[0] = gk_piece(0)


    for k in order[3::-1]:
        project(k)

    for hh in range(2):
        for e in range(1, 8):
            copy_to(gps.at[0], gpr.at[e, hh], gp_s.at[0], gp_r.at[e, hh], ddev((d + e) % 8)).wait_recv()
        acc = gpo[hh]
        for e in range(1, 8):
            acc = acc + gpr[e, hh].astype(F32)
        gsum[96 * hh : 96 * (hh + 1), :] = acc
        gsb[96 * hh : 96 * (hh + 1), :] = acc.astype(BF16)

    att_ref[...] = att_acc[...].astype(BF16)

    def share(i):
        return pl.ds(pl.multiple_of(16 * i, 16), 16)

    def ps_copy(o):
        i = (s + o) % 16
        return copy_to(gsb.at[share(i)], prr.at[o], ps_s.at[o], ps_r.at[o], {"seq": i})

    def as_copy(o, source):
        rows16 = gpf.at[d, share(source)]
        return copy_to(rows16, rows16, as_s.at[o], as_r.at[o], {"seq": (s + o) % 16})

    for o in range(1, 16):

        @pl.when((s + o) % 16 < 12)
        def _():
            ps_copy(o).start()

    @pl.when(s < 12)
    def _():
        acc = gsum[share(s), :]
        for o in range(1, 16):
            copy_to(gsb.at[0:16], prr.at[o], ps_s.at[o], ps_r.at[o], {"seq": (s + o) % 16}).wait_recv()
            acc = acc + prr[o].astype(F32)
        gpf[d, share(s), :] = acc.astype(BF16)
        for o in range(1, 16):
            as_copy(o, s).start()

    def ad_copy(e, source):
        return copy_to(gpf.at[d], gpf.at[source], ad_s.at[e], ad_r.at[e], ddev((d + 2 * e) % 8))

    def ac_copy(e, mine, other):
        return copy_to(gpf.at[mine], gpf.at[other], ac_s.at[e], ac_r.at[e], ddev(d + 1 - 2 * core))

    def ac_source(e):
        return (d - 2 * e + 8) % 8

    for o in range(1, 16):
        source = (s - o + 16) % 16

        @pl.when(source < 12)
        def _():
            as_copy(o, source).wait_recv()

    for e in (2, 1, 3):
        ad_copy(e, d).start()
    ac_copy(0, d, d).start()

    for k in order:
        gq_copy(k).wait_recv()
        gk_copy(k).wait_recv()

    for group in range(4):
        lanes = pl.ds(CW * group, CW)
        slots = [(4 * group + i - z + 16) % 16 for i in range(4)]
        queries = [unpack(gqr[t].astype(F32)) for t in slots]
        pairs = [unpack(gkr[t].astype(F32)) for t in slots]
        gq_ref[:, lanes] = jnp.concatenate(queries, axis=1).astype(BF16)
        gk_ref[:, lanes] = jnp.concatenate([p[0:40] for p in pairs], axis=1).astype(BF16)
        gv_ref[:, lanes] = jnp.concatenate([p[40:80] for p in pairs], axis=1).astype(BF16)

    for e in (1, 3, 2):
        ad_copy(e, ac_source(e)).wait_recv()
        ac_copy(e, ac_source(e), ac_source(e)).start()
    sibling = d + 1 - 2 * core
    for e in range(4):
        ac_copy(e, d, (sibling - 2 * e + 8) % 8).wait_recv()
    for i in range(8):
        gp_ref[192 * i : 192 * (i + 1), :] = gpf[i]

    for j in range(1, 4):
        zkv_copy(j).wait_send()
        zq_copy(j).wait_send()
    for xo in range(1, 4):
        for j in range(4):
            xkv_copy(xo, j).wait_send()
            rs_copy(xo * 4 + j).wait_send()
    for k in range(1, 16):
        gc_copy(k).wait_send()
        ctx_copy(k).wait_send()
        gq_copy(k).wait_send()
        gk_copy(k).wait_send()
    for k in range(16):

        @pl.when(owner(k)[0] != d)
        def _():
            gp_copy(k).wait_send()

    for o in range(1, 16):

        @pl.when((s + o) % 16 < 12)
        def _():
            ps_copy(o).wait_send()

    @pl.when(s < 12)
    def _():
        for o in range(1, 16):
            as_copy(o, s).wait_send()

    for e in range(1, 4):
        ad_copy(e, d).wait_send()
    for e in range(4):
        ac_copy(e, ac_source(e), ac_source(e)).wait_send()


def per_device(query, key, value, proj_weight, grad_out):
    vmem = pl.BlockSpec(memory_space=pltpu.VMEM)
    dma = pltpu.SemaphoreType.DMA
    width = query.shape[2]
    outs = pl.pallas_call(
        kernel,
        out_shape=(
            jax.ShapeDtypeStruct((FR, CW), BF16),
            jax.ShapeDtypeStruct((40, width), BF16),
            jax.ShapeDtypeStruct((40, width), BF16),
            jax.ShapeDtypeStruct((40, width), BF16),
            jax.ShapeDtypeStruct((width, CW), BF16),
        ),
        in_specs=[pl.BlockSpec(memory_space=pltpu.HBM)] * 5,
        out_specs=(vmem,) * 5,
        scratch_shapes=[
            pltpu.VMEM((FR, width), BF16),
            pltpu.VMEM((FR, width), BF16),
            pltpu.VMEM((FR, width), BF16),
            pltpu.VMEM((width, CW), BF16),
            pltpu.VMEM((FR, CW), BF16),
            pltpu.VMEM((4, 128, 128), BF16),
            pltpu.VMEM((4, 240, 128), BF16),
            pltpu.VMEM((4, 128, 128), BF16),
            pltpu.VMEM((QN, HD), BF16),
            pltpu.VMEM((16, 240, 128), BF16),
            pltpu.VMEM((16, FR, HD), BF16),
            pltpu.VMEM((16, 128, 128), BF16),
            pltpu.VMEM((16, 128, 128), BF16),
            pltpu.VMEM((16, 128, 128), BF16),
            pltpu.VMEM((QN, HD), BF16),
            pltpu.VMEM((16, FR, QN), F32),
            pltpu.VMEM((16, 1, QN), F32),
            pltpu.VMEM((HD, QN), F32),
            pltpu.VMEM((4, 128, 128), BF16),
            pltpu.VMEM((16, 128, 128), BF16),
            pltpu.VMEM((HD, QN), F32),
            pltpu.VMEM((QN, HD), F32),
            pltpu.VMEM((16, 240, 128), BF16),
            pltpu.VMEM((16, 240, 128), BF16),
            pltpu.VMEM((4, 240, 128), F32),
            pltpu.VMEM((4, FR, HD), F32),
            pltpu.VMEM((4, FR, HD), F32),
            pltpu.VMEM((16, 32, 128), BF16),
            pltpu.VMEM((16, 32, 128), BF16),
            pltpu.VMEM((16, 64, 128), BF16),
            pltpu.VMEM((16, 64, 128), BF16),
            pltpu.VMEM((FR, CW), F32),
            pltpu.VMEM((16, HD, CW), BF16),
            pltpu.VMEM((8, 2, HD, CW), BF16),
            pltpu.VMEM((2, HD, CW), F32),
            pltpu.VMEM((192, CW), F32),
            pltpu.VMEM((192, CW), BF16),
            pltpu.VMEM((16, 16, CW), BF16),
            pltpu.VMEM((8, 192, CW), BF16),
            dma((4,)), dma((4,)),
            dma((4,)), dma((4,)),
            dma((16,)), dma((16,)),
            dma((16,)), dma((16,)),
            dma((16,)), dma((16,)),
            dma((16,)), dma((16,)),
            dma((16,)), dma((16,)),
            dma((16,)), dma((16,)),
            dma((16,)), dma((8, 2)),
            dma((16,)), dma((16,)),
            dma((16,)), dma((16,)),
            dma((4,)), dma((4,)),
            dma((4,)), dma((4,)),
            dma((5,)),
        ],
        compiler_params=pltpu.CompilerParams(
            collective_id=0, has_side_effects=True, vmem_limit_bytes=64 * 1024 * 1024 - 65536
        ),
        name="attention",
    )(query[0], key[0], value[0], proj_weight, grad_out[0])
    att, gq, gk, gv, gp = outs
    return att[None], gq[None], gk[None], gv[None], gp


def solution(mesh):
    return jax.shard_map(
        per_device,
        mesh=mesh,
        in_specs=(
            P("dp", "seq", None),
            P("dp", "seq", None),
            P("dp", "seq", None),
            P(None, "mp"),
            P("dp", "seq", "mp"),
        ),
        out_specs=(
            P("dp", "seq", "mp"),
            P("dp", ("seq", "mp"), None),
            P("dp", ("seq", "mp"), None),
            P("dp", ("seq", "mp"), None),
            P(None, "mp"),
        ),
        check_vma=False,
    )
```

```python
import math

import jax
import jax.numpy as jnp
from jax import lax
from jax.experimental import pallas as pl
from jax.experimental.pallas import tpu as pltpu
from jax.sharding import PartitionSpec as P

MESH = pl.DeviceIdType.MESH
F32 = jnp.float32
BF16 = jnp.bfloat16
HD = 96
SCALE = 1.0 / math.sqrt(HD)
EXP2_SCALE = SCALE * math.log2(math.e)
NT = (((1,), (1,)), ((), ()))
NN = (((1,), (0,)), ((), ()))
TN = (((0,), (0,)), ((), ()))
FR = 160
QN = 640
CW = 384


def dot(a, b, dims):
    return lax.dot_general(a, b, dims, preferred_element_type=F32)


def pack(block):
    t = block.shape[0] // 5
    tail = block[4 * t :, :]
    side = jnp.concatenate(
        [tail[:, 0:32], tail[:, 32:64], tail[:, 64:96], jnp.zeros((t, 32), block.dtype)], axis=0
    )
    return jnp.concatenate([block[: 4 * t, :], side], axis=1)


def unpack(block):
    t = block.shape[0] // 4
    side = block[:, 96:128]
    tail = jnp.concatenate([side[0:t], side[t : 2 * t], side[2 * t : 3 * t]], axis=1)
    return jnp.concatenate([block[:, 0:96], tail], axis=0)


def pack_pair(a, b):
    low = jnp.concatenate([b[0:80, 32:96], b[80:160, 32:96]], axis=1)
    return jnp.concatenate([jnp.concatenate([a, b[:, 0:32]], axis=1), low], axis=0)


def unpack_pair(block):
    low = jnp.concatenate([block[160:240, 0:64], block[160:240, 64:128]], axis=0)
    return block[0:160, 0:96], jnp.concatenate([block[0:160, 96:128], low], axis=1)


def copy_to(src, dst, send, recv, device):
    return pltpu.make_async_remote_copy(
        src_ref=src, dst_ref=dst, send_sem=send, recv_sem=recv, device_id=device, device_id_type=MESH
    )


def kernel(
    q_hbm, k_hbm, v_hbm, w_hbm, go_hbm,
    att_ref, gq_ref, gk_ref, gv_ref, gp_ref,
    q_ref, k_ref, v_ref, w_ref, go_ref,
    zsq, zskv, qin, qbuf, kvbuf, vbuf, gcs, gcm, gcr, gall, scores, tops, ctxt, ctxs, ctxr, dqt, dqf, rss, rsr, own_kv, gk_all, gv_all,
    gqs, gqr, gks, gkr, att_acc, gps, gpr, gpo, gsum, gsb, prr, gpf,
    zq_s, zq_r, zkv_s, zkv_r, xkv_s, xkv_r, gc_s, gc_r, ctx_s, ctx_r, rs_s, rs_r,
    gq_s, gq_r, gk_s, gk_r, gp_s, gp_r, ps_s, ps_r, as_s, as_r, ad_s, ad_r, ac_s, ac_r, in_s,
):
    d = lax.axis_index("dp")
    s = lax.axis_index("seq")
    m = lax.axis_index("mp")
    x = s // 4
    zl = s % 4
    z = m * 4 + zl
    core = d % 2

    def zdev(zz):
        return {"seq": x * 4 + zz % 4, "mp": zz // 4}

    def xdev(xx):
        return {"seq": xx * 4 + zl}

    def ddev(dd):
        return {"dp": dd}

    barrier = pltpu.get_barrier_semaphore()
    for k in range(1, 16):
        pl.semaphore_signal(barrier, inc=1, device_id=zdev((z + k) % 16), device_id_type=MESH)
    for k in range(1, 4):
        for i in range(4):
            row = {"seq": (x + k) % 4 * 4 + (zl + i) % 4}
            pl.semaphore_signal(barrier, inc=1, device_id=row, device_id_type=MESH)
    for k in range(1, 8):
        pl.semaphore_signal(barrier, inc=1, device_id=ddev((d + k) % 8), device_id_type=MESH)

    fetches = [
        pltpu.make_async_copy(src, dst, in_s.at[i])
        for i, (src, dst) in enumerate(
            ((k_hbm, k_ref), (v_hbm, v_ref), (q_hbm, q_ref), (w_hbm, w_ref), (go_hbm, go_ref))
        )
    ]
    for fetch in fetches:
        fetch.start()

    def offset(j):
        return (0, 1, 2 - 4 * core, -1)[j]

    def head_of(j):
        return (z + offset(j) + 16) % 16

    rows = lax.broadcasted_iota(jnp.int32, (CW, HD), 0)
    cols = lax.broadcasted_iota(jnp.int32, (CW, HD), 1)
    wide_rows = lax.broadcasted_iota(jnp.int32, (CW, 128), 0)
    wide_cols = lax.broadcasted_iota(jnp.int32, (CW, 128), 1)

    def wide_pick(start, lane, count):
        inside = (wide_cols >= lane) & (wide_cols < lane + count)
        return jnp.where((wide_rows - start == wide_cols - lane) & inside, 1.0, 0.0).astype(BF16)

    def window(h):
        return pl.ds(pl.multiple_of(CW * (h // 4), 128), CW)

    fetches[0].wait()
    fetches[1].wait()
    for j in (1, 3, 2, 0):
        h = head_of(j)
        start = HD * (h % 4)
        kh = k_ref[:, window(h)]
        vh = v_ref[:, window(h)]
        top_part = dot(kh, wide_pick(start, 0, 96), NN) + dot(vh, wide_pick(start, 96, 32), NN)
        low_part = dot(vh[0:80], wide_pick(start + 32, 0, 64), NN) + dot(
            vh[80:160], wide_pick(start + 32, 64, 64), NN
        )
        if j == 0:
            kvbuf[0, 0:160, :] = top_part.astype(BF16)
            kvbuf[0, 160:240, :] = low_part.astype(BF16)
        else:
            zskv[j, 0:160, :] = top_part.astype(BF16)
            zskv[j, 160:240, :] = low_part.astype(BF16)

    pl.semaphore_wait(barrier, 34)

    def zkv_copy(j):
        return copy_to(zskv.at[j], kvbuf.at[j], zkv_s.at[j], zkv_r.at[j], zdev(head_of(j)))

    def zq_copy(j):
        return copy_to(zsq.at[j], qin.at[j], zq_s.at[j], zq_r.at[j], zdev(head_of(j)))

    def xkv_copy(xo, j):
        slot = xo * 4 + j
        return copy_to(kvbuf.at[j], kvbuf.at[slot], xkv_s.at[slot], xkv_r.at[slot], xdev((x + xo) % 4))

    for j in (1, 3, 2):
        zkv_copy(j).start()
    for xo in (2, 1, 3):
        xkv_copy(xo, 0).start()
    fetches[2].wait()
    for j in (1, 3, 2, 0):
        h = head_of(j)
        pick = jnp.where(rows - cols == HD * (h % 4), 1.0, 0.0).astype(BF16)
        qh = dot(q_ref[:, window(h)], pick, NN)
        if j == 0:
            qbuf[0:FR, :] = qh.astype(BF16)
        else:
            zsq[j] = pack(qh).astype(BF16)
            zq_copy(j).start()
    fetches[3].wait()
    fetches[4].wait()

    def gc_copy(k):
        if 5 <= k <= 11:
            step = 4 if k <= 8 else -4
            return copy_to(gcs.at[k], gcm.at[k], gc_s.at[k], gc_r.at[k], zdev((z + step + 16) % 16))
        return copy_to(gcs.at[k], gcr.at[k], gc_s.at[k], gc_r.at[k], zdev((z + k) % 16))

    def gc_relay():
        for k in (4, 3, 13, 2, 14, 1, 15):
            far = k + 4 if k < 8 else k - 4
            gc_copy(far).wait_recv()
            gcs[k] = (gcs[k].astype(F32) + gcm[far].astype(F32)).astype(BF16)
            gc_copy(k).start()

    def gc_step(k):
        h = (z + k) % 16
        part = dot(go_ref[...], w_ref[pl.ds(pl.multiple_of(HD * h, 32), HD), :], NT)
        gcs[k] = pack(part).astype(BF16)

    order = (8, 7, 9, 6, 10, 5, 11, 4, 12, 3, 13, 2, 14, 1, 15)
    for k in order[:5]:
        gc_step(k)
    for j in (1, 3, 2):
        zkv_copy(j).wait_recv()
        for xo in (2, 1, 3):
            xkv_copy(xo, j).start()
    for k in order[:5]:
        gc_copy(k).start()
    for k in order[5:]:
        gc_step(k)
        if 5 <= k <= 12:
            gc_copy(k).start()
    gcs[0] = pack(dot(go_ref[...], w_ref[pl.ds(pl.multiple_of(HD * z, 32), HD), :], NT)).astype(BF16)

    for j in (1, 3, 2):
        zq_copy(j).wait_recv()
        qbuf[FR * j : FR * (j + 1), :] = unpack(qin[j].astype(F32)).astype(BF16)

    ctxt[...] = jnp.zeros_like(ctxt)

    def score_slot(slot, carry):
        top, total = carry
        keys, values = unpack_pair(kvbuf[slot].astype(F32))
        values = values.astype(BF16)
        vbuf[slot] = values
        block = dot(keys.astype(BF16), qbuf[...], NT)
        new_top = jnp.maximum(top, jnp.max(block, axis=0, keepdims=True))
        keep = jnp.exp2((top - new_top) * EXP2_SCALE)
        p = jnp.exp2((block - new_top) * EXP2_SCALE)
        scores[slot] = p
        tops[slot] = new_top
        ctxt[...] = ctxt[...] * keep + dot(values, p.astype(BF16), TN)
        return new_top, total * keep + jnp.sum(p.reshape(FR // 8, 8, QN), axis=0)

    carry = (jnp.full((1, QN), -jnp.inf, F32), jnp.zeros((8, QN), F32))
    carry = lax.fori_loop(0, 4, score_slot, carry)
    for xo in (1, 3, 2):
        for j in (0, 1, 3, 2):
            xkv_copy(xo, j).wait_recv()
            carry = score_slot(xo * 4 + j, carry)
        if xo == 1:
            gc_relay()
    row_top, total = carry
    inverse = 1.0 / jnp.sum(total, axis=0, keepdims=True)
    wide = ctxt[...] * inverse
    ctxt[...] = wide
    narrow = wide.T
    for j in range(4):
        ctxs[j] = pack(narrow[j * FR : (j + 1) * FR, :]).astype(BF16)

    def ctx_copy(k):
        if 5 <= k <= 11:
            source, step = (ctxr.at[k - 4], -4) if k <= 8 else (ctxr.at[k + 4], 4)
        else:
            source, step = ctxs.at[k % 4], -k
        return copy_to(source, ctxr.at[k], ctx_s.at[k], ctx_r.at[k], zdev((z + step + 16) % 16))

    for k in (4, 12, 3, 13, 2, 14, 1, 15):
        ctx_copy(k).start()
    ctxr[0] = ctxs[0]

    for j in range(4):
        acc = gcs[0].astype(F32) if j == 0 else None
        for k in (4, 12) if j == 0 else (j, j + 12):
            gc_copy(k).wait_recv()
            part = gcr[k].astype(F32)
            acc = part if acc is None else acc + part
        gall[j * FR : (j + 1) * FR, :] = unpack(acc).astype(BF16)
    for k in (4, 3, 13, 2, 14, 1, 15):
        ctx_copy(k).wait_recv()
        ctx_copy(k + 4 if k < 8 else k - 4).start()
    delta = jnp.sum(gall[...].astype(F32).T * ctxt[...], axis=0, keepdims=True)

    att_acc[...] = jnp.zeros_like(att_acc)

    def owner(k):
        h = (z + k) % 16
        return h // 2, h % 2

    def gp_copy(k):
        dd, hh = owner(k)
        e = (dd - d + 8) % 8
        return copy_to(gps.at[k], gpr.at[e, hh], gp_s.at[k], gp_r.at[e, hh], ddev(dd))

    def project(k):
        if 5 <= k <= 12:
            ctx_copy(k).wait_recv()
        h = (z + k) % 16
        dd, hh = owner(k)
        context = unpack(ctxr[k].astype(F32)).astype(BF16)
        att_acc[...] += dot(context, w_ref[pl.ds(pl.multiple_of(HD * h, 32), HD), :], NN)
        part = dot(context, go_ref[...], TN)

        @pl.when(dd == d)
        def _():
            gpo[hh] = part

        @pl.when(dd != d)
        def _():
            gps[k] = part.astype(BF16)
            gp_copy(k).start()

    dqt[...] = jnp.zeros_like(dqt)

    def back_slot(slot):
        p = scores[slot] * (jnp.exp2((tops[slot] - row_top) * EXP2_SCALE) * inverse)
        gprob = dot(vbuf[slot], gall[...], NT)
        ds = (p * (gprob - delta) * SCALE).astype(BF16)
        dk = dot(ds, qbuf[...], NN)
        dv = dot(p.astype(BF16), gall[...], NN)
        dqt[...] += dot(kvbuf[slot, 0:160, 0:96], ds, TN)
        return pack_pair(dk, dv)

    def rs_copy(slot):
        xo = slot // 4
        return copy_to(rss.at[slot], rsr.at[slot], rs_s.at[slot], rs_r.at[slot], xdev((x - xo + 4) % 4))

    def away_slot(i, carry):
        slot = 15 - i
        rss[slot] = back_slot(slot).astype(BF16)
        rs_copy(slot).start()
        return carry

    lax.fori_loop(0, 12, away_slot, 0)
    project(0)
    for k in (15, 1, 14, 2, 13, 3):
        project(k)

    def own_slot(slot, carry):
        own_kv[slot] = back_slot(slot)
        return carry

    lax.fori_loop(0, 4, own_slot, 0)

    dqf[...] = dqt[...].T

    def gq_copy(k):
        return copy_to(gqs.at[k], gqr.at[k], gq_s.at[k], gq_r.at[k], zdev((z - k + 16) % 16))

    def gk_copy(k):
        return copy_to(gks.at[k], gkr.at[k], gk_s.at[k], gk_r.at[k], zdev((z - k + 16) % 16))

    def piece_start(k):
        return pl.multiple_of(40 * (((z - k + 16) % 16) // 4), 8)

    def gq_piece(k):
        return pack(dqf[pl.ds(FR * (k % 4) + piece_start(k), 40), :]).astype(BF16)

    for k in order:
        gqs[k] = gq_piece(k)
        gq_copy(k).start()
    gqr[0] = gq_piece(0)

    for k in (12, 4, 8, 7, 9):
        project(k)

    for j in range(4):
        for xo in (3, 2, 1):
            rs_copy(xo * 4 + j).wait_recv()
        summed = (
            own_kv[j] + rsr[4 + j].astype(F32) + rsr[8 + j].astype(F32) + rsr[12 + j].astype(F32)
        )
        gk_all[j], gv_all[j] = unpack_pair(summed)

    def gk_piece(k):
        rows40 = pl.ds(piece_start(k), 40)
        return pack(
            jnp.concatenate([gk_all[k % 4, rows40, :], gv_all[k % 4, rows40, :]], axis=0)
        ).astype(BF16)

    for k in order:
        gks[k] = gk_piece(k)
        gk_copy(k).start()
    gkr[0] = gk_piece(0)


    for k in (6, 10, 5, 11):
        project(k)

    for hh in range(2):
        for e in range(1, 8):
            copy_to(gps.at[0], gpr.at[e, hh], gp_s.at[0], gp_r.at[e, hh], ddev((d + e) % 8)).wait_recv()
        acc = gpo[hh]
        for e in range(1, 8):
            acc = acc + gpr[e, hh].astype(F32)
        gsum[96 * hh : 96 * (hh + 1), :] = acc
        gsb[96 * hh : 96 * (hh + 1), :] = acc.astype(BF16)

    att_ref[...] = att_acc[...].astype(BF16)

    def share(i):
        return pl.ds(pl.multiple_of(16 * i, 16), 16)

    def ps_copy(o):
        i = (s + o) % 16
        return copy_to(gsb.at[share(i)], prr.at[o], ps_s.at[o], ps_r.at[o], {"seq": i})

    def as_copy(o, source):
        rows16 = gpf.at[d, share(source)]
        return copy_to(rows16, rows16, as_s.at[o], as_r.at[o], {"seq": (s + o) % 16})

    for o in range(1, 16):

        @pl.when((s + o) % 16 < 12)
        def _():
            ps_copy(o).start()

    @pl.when(s < 12)
    def _():
        acc = gsum[share(s), :]
        for o in range(1, 16):
            copy_to(gsb.at[0:16], prr.at[o], ps_s.at[o], ps_r.at[o], {"seq": (s + o) % 16}).wait_recv()
            acc = acc + prr[o].astype(F32)
        gpf[d, share(s), :] = acc.astype(BF16)
        for o in range(1, 16):
            as_copy(o, s).start()

    def ad_copy(e, source):
        return copy_to(gpf.at[d], gpf.at[source], ad_s.at[e], ad_r.at[e], ddev((d + 2 * e) % 8))

    def ac_copy(e, mine, other):
        return copy_to(gpf.at[mine], gpf.at[other], ac_s.at[e], ac_r.at[e], ddev(d + 1 - 2 * core))

    def ac_source(e):
        return (d - 2 * e + 8) % 8

    for o in range(1, 16):
        source = (s - o + 16) % 16

        @pl.when(source < 12)
        def _():
            as_copy(o, source).wait_recv()

    for e in (2, 1, 3):
        ad_copy(e, d).start()
    ac_copy(0, d, d).start()

    for k in order:
        gq_copy(k).wait_recv()
        gk_copy(k).wait_recv()

    for group in range(4):
        lanes = pl.ds(CW * group, CW)
        slots = [(4 * group + i - z + 16) % 16 for i in range(4)]
        queries = [unpack(gqr[t].astype(F32)) for t in slots]
        pairs = [unpack(gkr[t].astype(F32)) for t in slots]
        gq_ref[:, lanes] = jnp.concatenate(queries, axis=1).astype(BF16)
        gk_ref[:, lanes] = jnp.concatenate([p[0:40] for p in pairs], axis=1).astype(BF16)
        gv_ref[:, lanes] = jnp.concatenate([p[40:80] for p in pairs], axis=1).astype(BF16)

    for e in (1, 3, 2):
        ad_copy(e, ac_source(e)).wait_recv()
        ac_copy(e, ac_source(e), ac_source(e)).start()
    sibling = d + 1 - 2 * core
    for e in range(4):
        ac_copy(e, d, (sibling - 2 * e + 8) % 8).wait_recv()
    for i in range(8):
        gp_ref[192 * i : 192 * (i + 1), :] = gpf[i]

    for j in range(1, 4):
        zkv_copy(j).wait_send()
        zq_copy(j).wait_send()
    for xo in range(1, 4):
        for j in range(4):
            xkv_copy(xo, j).wait_send()
            rs_copy(xo * 4 + j).wait_send()
    for k in range(1, 16):
        gc_copy(k).wait_send()
        ctx_copy(k).wait_send()
        gq_copy(k).wait_send()
        gk_copy(k).wait_send()
    for k in range(16):

        @pl.when(owner(k)[0] != d)
        def _():
            gp_copy(k).wait_send()

    for o in range(1, 16):

        @pl.when((s + o) % 16 < 12)
        def _():
            ps_copy(o).wait_send()

    @pl.when(s < 12)
    def _():
        for o in range(1, 16):
            as_copy(o, s).wait_send()

    for e in range(1, 4):
        ad_copy(e, d).wait_send()
    for e in range(4):
        ac_copy(e, ac_source(e), ac_source(e)).wait_send()


def per_device(query, key, value, proj_weight, grad_out):
    vmem = pl.BlockSpec(memory_space=pltpu.VMEM)
    dma = pltpu.SemaphoreType.DMA
    width = query.shape[2]
    outs = pl.pallas_call(
        kernel,
        out_shape=(
            jax.ShapeDtypeStruct((FR, CW), BF16),
            jax.ShapeDtypeStruct((40, width), BF16),
            jax.ShapeDtypeStruct((40, width), BF16),
            jax.ShapeDtypeStruct((40, width), BF16),
            jax.ShapeDtypeStruct((width, CW), BF16),
        ),
        in_specs=[pl.BlockSpec(memory_space=pltpu.HBM)] * 5,
        out_specs=(vmem,) * 5,
        scratch_shapes=[
            pltpu.VMEM((FR, width), BF16),
            pltpu.VMEM((FR, width), BF16),
            pltpu.VMEM((FR, width), BF16),
            pltpu.VMEM((width, CW), BF16),
            pltpu.VMEM((FR, CW), BF16),
            pltpu.VMEM((4, 128, 128), BF16),
            pltpu.VMEM((4, 240, 128), BF16),
            pltpu.VMEM((4, 128, 128), BF16),
            pltpu.VMEM((QN, HD), BF16),
            pltpu.VMEM((16, 240, 128), BF16),
            pltpu.VMEM((16, FR, HD), BF16),
            pltpu.VMEM((16, 128, 128), BF16),
            pltpu.VMEM((16, 128, 128), BF16),
            pltpu.VMEM((16, 128, 128), BF16),
            pltpu.VMEM((QN, HD), BF16),
            pltpu.VMEM((16, FR, QN), F32),
            pltpu.VMEM((16, 1, QN), F32),
            pltpu.VMEM((HD, QN), F32),
            pltpu.VMEM((4, 128, 128), BF16),
            pltpu.VMEM((16, 128, 128), BF16),
            pltpu.VMEM((HD, QN), F32),
            pltpu.VMEM((QN, HD), F32),
            pltpu.VMEM((16, 240, 128), BF16),
            pltpu.VMEM((16, 240, 128), BF16),
            pltpu.VMEM((4, 240, 128), F32),
            pltpu.VMEM((4, FR, HD), F32),
            pltpu.VMEM((4, FR, HD), F32),
            pltpu.VMEM((16, 32, 128), BF16),
            pltpu.VMEM((16, 32, 128), BF16),
            pltpu.VMEM((16, 64, 128), BF16),
            pltpu.VMEM((16, 64, 128), BF16),
            pltpu.VMEM((FR, CW), F32),
            pltpu.VMEM((16, HD, CW), BF16),
            pltpu.VMEM((8, 2, HD, CW), BF16),
            pltpu.VMEM((2, HD, CW), F32),
            pltpu.VMEM((192, CW), F32),
            pltpu.VMEM((192, CW), BF16),
            pltpu.VMEM((16, 16, CW), BF16),
            pltpu.VMEM((8, 192, CW), BF16),
            dma((4,)), dma((4,)),
            dma((4,)), dma((4,)),
            dma((16,)), dma((16,)),
            dma((16,)), dma((16,)),
            dma((16,)), dma((16,)),
            dma((16,)), dma((16,)),
            dma((16,)), dma((16,)),
            dma((16,)), dma((16,)),
            dma((16,)), dma((8, 2)),
            dma((16,)), dma((16,)),
            dma((16,)), dma((16,)),
            dma((4,)), dma((4,)),
            dma((4,)), dma((4,)),
            dma((5,)),
        ],
        compiler_params=pltpu.CompilerParams(
            collective_id=0, has_side_effects=True, vmem_limit_bytes=64 * 1024 * 1024 - 65536
        ),
        name="attention",
    )(query[0], key[0], value[0], proj_weight, grad_out[0])
    att, gq, gk, gv, gp = outs
    return att[None], gq[None], gk[None], gv[None], gp


def solution(mesh):
    return jax.shard_map(
        per_device,
        mesh=mesh,
        in_specs=(
            P("dp", "seq", None),
            P("dp", "seq", None),
            P("dp", "seq", None),
            P(None, "mp"),
            P("dp", "seq", "mp"),
        ),
        out_specs=(
            P("dp", "seq", "mp"),
            P("dp", ("seq", "mp"), None),
            P("dp", ("seq", "mp"), None),
            P("dp", ("seq", "mp"), None),
            P(None, "mp"),
        ),
        check_vma=False,
    )
```
